32 devices in a mesh: groups: 2 (over y), store: 4 (over z), head: 2 (over x), pair: 2 (over core).
Axes of the slice: x: 2, y: 2, z: 4, core: 2. Of those that a mesh axis runs over, the one named last changes fastest.
Arguments:
- passage_cache: bfloat16 [128, 8, 2, 512, 128], P(('groups', 'store', 'pair'), 'head'), parts along dimension 0, may hold values from -6 to 6
- queries: bfloat16 [16, 32, 24, 64, 128], P(('groups', 'store', 'pair'), None, None, 'head'), parts along dimension 0, may hold values from -64 to 64
- passage_home: int32 [128], P('groups'), parts along dimension 0, may hold values from 0 to 63, as said below
- retrieval: int32 [16, 32], P(('groups', 'store', 'pair')), parts along dimension 0, may hold values from 0 to 63, as said below
- counts: int32 [16], P(('groups', 'store', 'pair')), parts along dimension 0, may hold values from 8 to 32, as said below
- boundary_rows: int32 [16, 32, 24], P(('groups', 'store', 'pair')), parts along dimension 0, may hold values from 0 to 511, as said below
- cross_blocks: int32 [16, 32, 2], P(('groups', 'store', 'pair')), parts along dimension 0, may hold values from 0 to 31, as said below
Outputs:
- attended: bfloat16 [16, 32, 24, 64, 128], P(('groups', 'store', 'pair'), None, None, 'head'), parts along dimension 0
The draws below stay inside these ranges and needn't reach their ends.
There are 2 independent parts, one for each index of `groups`. The reference program is written for one: setup_inputs(seed, part) draws one part's arguments, and reference() takes and returns one part's arrays. A program takes and returns all parts, laid end to end along the dimension named above; each array names one. Nothing has to cross between parts.
Inputs may be any that keep to these rules, and one draw needn't show every extreme that they name: `passage_home`: a permutation: each passage has one row of passage_cache, and rows s * 8 to (s + 1) * 8 - 1 form cache shard s. `retrieval`: the ids of one request are distinct; among its live slots at most 4 lie on one cache shard, and the request with 32 live slots has exactly 4 on every shard; ids in slots from counts[r] on are never read. `counts`: some request has 32 live slots. `boundary_rows`: distinct and rising within one slot. `cross_blocks`: an entry of slot j is an earlier slot or j itself, which stands for no passage; the earlier slots listed for one slot are distinct.
All inputs are finite; a program needn't handle non-finite values.
Results may differ from the reference program's by a relative error of at most 0.0034.
Values may be sent and summed in bfloat16 or wider, within the bound.
A program may use at most 192 MiB of HBM per device.

```python
import jax
import jax.numpy as jnp
from jax import lax

HEADS = 64
KV_HEADS = 8
HD = 128
PLEN = 512
MAXC = 32
MINC = 8
WB = 2
BR = 24
PASS_DEV = 8
SHARDS = 8
REQUESTS = 8
PASSAGES = 64


def placement_tables(key):
    home_rows = jax.random.permutation(jax.random.fold_in(key, 101), PASSAGES).astype(jnp.int32)
    inverse = jnp.argsort(home_rows).astype(jnp.int32)
    slot_scores = jax.random.randint(jax.random.fold_in(key, 102), (REQUESTS, MAXC), 0, 1 << 20) * MAXC + jnp.arange(MAXC, dtype=jnp.int32)[None, :]
    slot_order = jnp.argsort(slot_scores, axis=1).astype(jnp.int32)
    shard_id = slot_order % SHARDS
    order_rank = slot_order // SHARDS
    offsets = jax.random.randint(jax.random.fold_in(key, 103), (REQUESTS, SHARDS), 0, PASS_DEV)
    offset_pick = jnp.take_along_axis(offsets, shard_id, axis=1)
    local_row = (order_rank + offset_pick) % PASS_DEV
    chosen = inverse[shard_id * PASS_DEV + local_row]
    return (home_rows, chosen.astype(jnp.int32))


def draw_passage_home(key, part):
    return placement_tables(key)[0]


def draw_retrieval(key, part):
    return placement_tables(key)[1]


def draw_counts(key, part):
    key = jax.random.fold_in(key, 3)
    parts_key = jax.random.split(key, 4)
    first = jax.random.randint(parts_key[0], (REQUESTS,), 0, MAXC - MINC + 1)
    second = jax.random.randint(parts_key[1], (REQUESTS,), 0, MAXC - MINC + 1)
    third = jax.random.randint(parts_key[2], (REQUESTS,), 0, MAXC - MINC + 1)
    result = MINC + jnp.minimum(first, jnp.minimum(second, third))
    fullest = jax.random.randint(parts_key[3], (), 0, REQUESTS)
    return result.at[fullest].set(MAXC).astype(jnp.int32)


def draw_boundary_rows(key, part):
    key = jax.random.fold_in(key, 4)
    row_scores = jax.random.randint(key, (REQUESTS, MAXC, PLEN), 0, 1 << 20) * PLEN + jnp.arange(PLEN, dtype=jnp.int32)
    picked = jnp.argsort(row_scores, axis=-1)[..., :BR]
    return jnp.sort(picked, axis=-1).astype(jnp.int32)


def draw_cross_blocks(key, part):
    key = jax.random.fold_in(key, 5)
    key_one, key_two = jax.random.split(key)
    slot_scores = jax.random.randint(key_one, (REQUESTS, MAXC, MAXC), 0, 1 << 20) * MAXC + jnp.arange(MAXC, dtype=jnp.int32)
    later = jnp.arange(MAXC, dtype=jnp.int32)[None, :] >= jnp.arange(MAXC, dtype=jnp.int32)[:, None]
    slot_scores = jnp.where(later[None], (1 << 26) + jnp.arange(MAXC, dtype=jnp.int32), slot_scores)
    picked = jnp.argsort(slot_scores, axis=-1)[..., :WB].astype(jnp.int32)
    own_slot = jnp.arange(MAXC, dtype=jnp.int32)[None, :, None]
    dropped = jax.random.randint(key_two, (REQUESTS, MAXC, WB), 0, 4) == 0
    picked = jnp.where((picked < own_slot) & jnp.logical_not(dropped), picked, own_slot)
    return picked.astype(jnp.int32)


def draw_passage_cache(key, part):
    key = jax.random.fold_in(key, 1)
    shape = (PASSAGES, KV_HEADS, 2, PLEN, HD)
    sample = jax.random.truncated_normal(key, -6.0, 6.0, shape, jnp.float32)
    return sample.astype(jnp.bfloat16)


def draw_queries(key, part):
    key = jax.random.fold_in(key, 2)
    shape = (REQUESTS, MAXC, BR, HEADS, HD)
    sample = 2.0 * jax.random.truncated_normal(key, -6.0, 6.0, shape, jnp.float32)
    return sample.astype(jnp.bfloat16)


def setup_inputs(seed: int = 0, part: int = 0) -> dict:
    keys = jax.random.split(jax.random.key(seed), 8)
    own_keys = jax.random.split(jax.random.fold_in(keys[7], part), 8)
    passage_cache = draw_passage_cache(jax.random.fold_in(jax.random.fold_in(keys[7], part), 71), part)
    queries = draw_queries(jax.random.fold_in(jax.random.fold_in(keys[7], part), 71), part)
    passage_home = draw_passage_home(jax.random.fold_in(jax.random.fold_in(keys[7], part), 71), part)
    retrieval = draw_retrieval(jax.random.fold_in(jax.random.fold_in(keys[7], part), 71), part)
    counts = draw_counts(jax.random.fold_in(jax.random.fold_in(keys[7], part), 71), part)
    boundary_rows = draw_boundary_rows(jax.random.fold_in(jax.random.fold_in(keys[7], part), 71), part)
    cross_blocks = draw_cross_blocks(jax.random.fold_in(jax.random.fold_in(keys[7], part), 71), part)
    return {"passage_cache": passage_cache, "queries": queries, "passage_home": passage_home, "retrieval": retrieval, "counts": counts, "boundary_rows": boundary_rows, "cross_blocks": cross_blocks}


def attend_slot(query_rows, own_block, others, row_list, link_list, slot_id):
    group_size = HEADS // KV_HEADS
    gathered = jnp.concatenate([own_block[None], others], axis=0).astype(jnp.float32)
    key_part = gathered[:, :, 0]
    value_part = gathered[:, :, 1]
    query_f32 = query_rows.astype(jnp.float32).reshape(BR, KV_HEADS, group_size, HD)
    scores = jnp.einsum('bkgd,wknd->kgbwn', query_f32, key_part) * (HD ** -0.5)
    position = jnp.arange(PLEN, dtype=jnp.int32)
    own_ok = position[None, :] <= row_list[:, None]
    link_ok = link_list != slot_id
    allowed = jnp.concatenate([own_ok[:, None, :], jnp.broadcast_to(link_ok[None, :, None], (BR, WB, PLEN))], axis=1)
    scores = jnp.where(allowed, scores, -jnp.inf)
    peak_score = jnp.max(scores, axis=(3, 4), keepdims=True)
    exp_scores = jnp.exp(scores - peak_score)
    totals = jnp.sum(exp_scores, axis=(3, 4))
    weights = lax.optimization_barrier(exp_scores.astype(jnp.bfloat16)).astype(jnp.float32)
    mixed_sum = jnp.einsum('kgbwn,wknd->bkgd', weights, value_part)
    result = mixed_sum / jnp.transpose(totals, (2, 0, 1))[..., None]
    return result.reshape(BR, HEADS, HD).astype(jnp.bfloat16)


def reference(passage_cache, queries, passage_home, retrieval, counts, boundary_rows, cross_blocks):
    def one_request(request_items):
        query_all, chosen, live_count, row_all, link_all = request_items
        places = passage_home[chosen]

        def one_slot(slot_id):
            def compute_slot():
                own_block = passage_cache[places[slot_id]]
                others = passage_cache[places[link_all[slot_id]]]
                return attend_slot(query_all[slot_id], own_block, others, row_all[slot_id], link_all[slot_id], slot_id)

            def empty_slot():
                return jnp.zeros((BR, HEADS, HD), jnp.bfloat16)

            return lax.cond(slot_id < live_count, compute_slot, empty_slot)

        return lax.map(one_slot, jnp.arange(MAXC, dtype=jnp.int32))

    return lax.map(one_request, (queries, retrieval, counts, boundary_rows, cross_blocks))
```

```python
import functools

import jax
import jax.numpy as jnp
from jax import lax
from jax.experimental import pallas as pl
from jax.experimental.pallas import tpu as pltpu
from jax.sharding import PartitionSpec as P

SLOTS_PER_STEP = 4
VMEM_BYTES = 48 * 1024 * 1024


def place_kernel(info, own_ref, sib_ref, buf_ref, sems):
    held = own_ref.shape[0]
    mine = pltpu.make_async_copy(own_ref, buf_ref.at[pl.ds(info[0] * held, held)], sems.at[0])
    other = pltpu.make_async_copy(sib_ref, buf_ref.at[pl.ds(info[1] * held, held)], sems.at[1])
    mine.start()
    other.start()
    mine.wait()
    other.wait()


def place_rows(info, own, sibling, rows):
    return pl.pallas_call(
        place_kernel,
        out_shape=jax.ShapeDtypeStruct((rows,) + own.shape[1:], own.dtype),
        grid_spec=pltpu.PrefetchScalarGridSpec(
            num_scalar_prefetch=1,
            grid=(),
            in_specs=[pl.BlockSpec(memory_space=pl.ANY)] * 2,
            out_specs=pl.BlockSpec(memory_space=pl.ANY),
            scratch_shapes=[pltpu.SemaphoreType.DMA((2,))],
        ),
    )(info, own, sibling)


def attend_kernel(br, span, order, place, extra, rows, q_ref, own_ref, one_ref, two_ref, prev_ref, out_ref):
    heads, total_rows, depth = q_ref.shape[1:]
    group = total_rows // br
    length = own_ref.shape[3]
    scale = depth ** (-0.5)
    step = pl.program_id(0)
    index = span[0] + step
    active = step < span[1]
    slot = order[jnp.minimum(index, order.shape[0] - 1)]
    live = jnp.logical_and(active, index < span[2])
    links = extra[slot]

    def run(kv_refs):
        position = lax.broadcasted_iota(jnp.int32, (group, length), 1)
        allowed = jnp.concatenate(
            [(position <= rows[slot * br + b]).astype(jnp.int32) for b in range(br)], axis=0
        ) > 0
        for h in range(heads):
            query = q_ref[0, h]
            scores = [
                lax.dot_general(
                    query, ref[0, h, 0], (((1,), (1,)), ((), ())), preferred_element_type=jnp.float32
                )
                for ref in kv_refs
            ]
            scores[0] = jnp.where(allowed, scores[0], -jnp.inf)
            peak = functools.reduce(jnp.maximum, scores)
            peak = jnp.max(peak, axis=1, keepdims=True)
            expon = [jnp.exp((s - peak) * scale) for s in scores]
            totals = jnp.sum(functools.reduce(jnp.add, expon), axis=1, keepdims=True)
            mixed = functools.reduce(
                jnp.add,
                [
                    jnp.dot(e.astype(jnp.bfloat16), ref[0, h, 1], preferred_element_type=jnp.float32)
                    for e, ref in zip(expon, kv_refs)
                ],
            )
            out_ref[0, h] = (mixed / totals).astype(out_ref.dtype)

    @pl.when(jnp.logical_and(live, links == 0))
    def _():
        run([own_ref])

    @pl.when(jnp.logical_and(live, links == 1))
    def _():
        run([own_ref, one_ref])

    @pl.when(jnp.logical_and(live, links == 2))
    def _():
        run([own_ref, one_ref, two_ref])

    @pl.when(jnp.logical_and(active, jnp.logical_not(live)))
    def _():
        out_ref[...] = jnp.zeros_like(out_ref)


def attend(steps, br, span, order, place, extra, rows, q, buf, prev):
    slots, heads, total_rows, depth = q.shape
    kv_block = (1,) + buf.shape[1:]

    def pick(k, span, order):
        index = jnp.minimum(span[0] + jnp.minimum(k, span[1] - 1), span[2] - 1)
        return order[jnp.clip(index, 0, slots - 1)]

    def q_map(k, span, order, place, extra, rows):
        return (pick(k, span, order), 0, 0, 0)

    def kv_map(which, k, span, order, place, extra, rows):
        return (place[pick(k, span, order) * 3 + which], 0, 0, 0, 0)

    def out_map(k, span, order, place, extra, rows):
        index = jnp.clip(span[0] + k, 0, slots - 1)
        return (jnp.where(k < span[1], order[index], slots), 0, 0, 0)

    return pl.pallas_call(
        functools.partial(attend_kernel, br),
        out_shape=jax.ShapeDtypeStruct(prev.shape, prev.dtype),
        grid_spec=pltpu.PrefetchScalarGridSpec(
            num_scalar_prefetch=5,
            grid=(steps,),
            in_specs=[pl.BlockSpec((1, heads, total_rows, depth), q_map)]
            + [pl.BlockSpec(kv_block, functools.partial(kv_map, w)) for w in range(3)]
            + [pl.BlockSpec(memory_space=pl.ANY)],
            out_specs=pl.BlockSpec((1, heads, total_rows, depth), out_map),
        ),
        input_output_aliases={9: 0},
        compiler_params=pltpu.CompilerParams(
            dimension_semantics=("arbitrary",), vmem_limit_bytes=VMEM_BYTES
        ),
        cost_estimate=pl.CostEstimate(
            flops=4 * steps * heads * total_rows * 3 * buf.shape[3] * depth,
            bytes_accessed=steps * 4 * heads * buf.shape[3] * depth * 6,
            transcendentals=steps * heads * total_rows * 3 * buf.shape[3],
        ),
    )(span, order, place, extra, rows, q, buf, buf, buf, prev)


def plan_links(need, held):
    chips = need.shape[2]
    dst = jnp.arange(chips)[:, None]
    src = jnp.arange(chips)[None, :]
    gap = jnp.where(src > dst, src - dst, 0)
    reach = jnp.max(jnp.where(need, gap[None, None, :, :, None, None], 0), axis=2)
    reach = jnp.swapaxes(reach, 2, 3)
    row = jnp.arange(held)
    ahead = (reach[..., None, :] > reach[..., :, None]) | (
        (reach[..., None, :] == reach[..., :, None]) & (row[None, :] < row[:, None])
    )
    rank = jnp.sum(ahead.astype(jnp.int32), axis=-1)
    start = jnp.zeros(reach.shape[:3] + (chips, chips), jnp.int32)
    last = None
    ends = []
    for d in range(1, chips):
        if last is None:
            now = jnp.zeros(reach.shape[:3] + (chips - 1,), jnp.int32)
        else:
            before = jnp.sum((reach >= d - 1).astype(jnp.int32), axis=-1)
            now = jnp.maximum(last[..., :-1] + before[..., d - 1 : chips - 1], last[..., 1:] + 2)
        sent = jnp.sum((reach >= d).astype(jnp.int32), axis=-1)[..., d:]
        ends.append(jnp.max(jnp.where(sent > 0, now + sent, 0)))
        wide = jnp.pad(now, [(0, 0)] * 3 + [(0, d)])
        start = jnp.where(src - dst == d, wide[..., :, None], start)
        last = now
    total = functools.reduce(jnp.maximum, ends, jnp.int32(0))
    time = start[..., None] + rank[:, :, :, None]
    used = (src > dst)[:, :, None] & (reach[:, :, :, None] >= (src - dst)[:, :, None])
    return jnp.where(used, time, -1), total


def local(passage_cache, queries, passage_home, retrieval, counts, boundary_rows, cross_blocks):
    groups = lax.axis_size("groups")
    chips = lax.axis_size("store")
    lanes = lax.axis_size("pair")
    my_group = lax.axis_index("groups")
    my_chip = lax.axis_index("store")
    my_lane = lax.axis_index("pair")
    held = passage_cache.shape[0]
    passages = passage_home.shape[0]
    slots = retrieval.shape[1]
    br = queries.shape[2]
    kv_heads = passage_cache.shape[1]
    group_size = queries.shape[3] // kv_heads
    depth = queries.shape[4]
    swap = [(i, (i + 1) % lanes) for i in range(lanes)]
    down = [(i + 1, i) for i in range(chips - 1)]
    up = [(i, i + 1) for i in range(chips - 1)]

    sibling = lax.ppermute(passage_cache, "pair", swap)
    my_shard = my_chip * lanes + my_lane
    sib_shard = my_chip * lanes + (my_lane + 1) % lanes
    buf = place_rows(jnp.stack([my_shard, sib_shard]).astype(jnp.int32), passage_cache, sibling, passages + 1)

    slot_ids = jnp.arange(slots, dtype=jnp.int32)
    live = slot_ids < counts[0]
    places = passage_home[retrieval[0]]
    hit = live[:, None] & (places[:, None] == jnp.arange(passages, dtype=jnp.int32)[None, :])
    needed = jnp.any(hit, axis=0).astype(jnp.int32)
    every = lax.all_gather(needed[None], ("groups", "store", "pair"), axis=0, tiled=True)
    need = jnp.max(every.reshape(groups, chips, lanes, passages), axis=2) > 0
    need = need.reshape(groups, chips, chips, lanes, held)
    time, total = plan_links(jnp.stack([need, need[:, ::-1, ::-1]]), held)

    my_time = lax.dynamic_index_in_dim(time, my_group, 1, keepdims=False)
    line = jnp.stack([my_chip, chips - 1 - my_chip])
    padded = jnp.pad(my_time, [(0, 0), (0, 0), (1, 0), (0, 0), (0, 0)], constant_values=-1)
    at_link = jnp.arange(chips + 1, dtype=jnp.int32)[None, :]
    select_in = (at_link == line[:, None] + 1)[:, None, :, None, None]
    select_out = (at_link == line[:, None])[:, None, :, None, None]
    time_in = jnp.max(jnp.where(select_in, padded, -1), axis=2)
    time_out = jnp.max(jnp.where(select_out, padded, -1), axis=2)
    home = jnp.arange(chips, dtype=jnp.int32)
    home = jnp.stack([home, chips - 1 - home])
    row_id = (
        (home[:, None, :, None] * lanes + jnp.arange(lanes, dtype=jnp.int32)[None, :, None, None]) * held
        + jnp.arange(held, dtype=jnp.int32)
    )
    most = (chips - 1) * max(held, 2) + 2
    steps = jnp.arange(most, dtype=jnp.int32)

    def table(when, empty):
        found = when[..., None] == steps
        value = jnp.sum(jnp.where(found, row_id[..., None] + 1, 0), axis=(2, 3)) - 1
        return jnp.where(value >= 0, value, empty)

    row_in = table(time_in, passages)
    row_out = table(time_out, my_shard * held)
    in_mine = lax.dynamic_index_in_dim(row_in, my_lane, 1, keepdims=False)
    in_sib = lax.dynamic_index_in_dim(row_in, (my_lane + 1) % lanes, 1, keepdims=False)
    out_mine = lax.dynamic_index_in_dim(row_out, my_lane, 1, keepdims=False)

    links = cross_blocks[0]
    valid = links != slot_ids[:, None]
    first = jnp.where(valid[:, 0], links[:, 0], links[:, 1])
    second = links[:, 1]
    count_links = jnp.sum(valid.astype(jnp.int32), axis=1)
    first = jnp.where(count_links >= 1, first, slot_ids)
    second = jnp.where(count_links >= 2, second, first)
    members = jnp.stack([slot_ids, first, second], axis=1)
    member_hit = (members[:, :, None] == slot_ids[None, None, :]) & live[None, None, :]
    member_place = jnp.sum(jnp.where(member_hit, places[None, None, :], 0), axis=2)
    arrival = jnp.max(
        jnp.where(
            (row_id[..., None] == jnp.arange(passages, dtype=jnp.int32)), time_in[..., None] + 1, 0
        ),
        axis=(0, 1, 2, 3),
    )
    slot_arrival = jnp.sum(jnp.where(hit, arrival[None, :], 0), axis=1)
    ready = jnp.max(jnp.where(member_hit, slot_arrival[None, None, :], 0), axis=(1, 2))
    ready = jnp.where(live, ready, most + 2)
    sooner = (ready[None, :] < ready[:, None]) | (
        (ready[None, :] == ready[:, None]) & (slot_ids[None, :] < slot_ids[:, None])
    )
    rank = jnp.sum(sooner.astype(jnp.int32), axis=1)
    order = jnp.sum(jnp.where(rank[None, :] == slot_ids[:, None], slot_ids[None, :], 0), axis=1)
    ready_count = jnp.sum((ready[None, :] <= steps[:, None]).astype(jnp.int32), axis=1)

    q = queries[0].reshape(slots, br, kv_heads, group_size, depth)
    q = jnp.transpose(q, (0, 2, 1, 3, 4)).reshape(slots, kv_heads, br * group_size, depth)
    rows = boundary_rows[0].reshape(-1)
    place = member_place.reshape(-1)
    out = jnp.zeros((slots + 1,) + q.shape[1:], q.dtype)

    def store(buf, block, row):
        return lax.dynamic_update_slice_in_dim(buf, block, row, 0)

    def load(buf, row):
        return lax.dynamic_slice_in_dim(buf, row, 1, 0)

    def take_in(t, buf, got_down, got_up):
        swap_down = lax.ppermute(got_down, "pair", swap)
        swap_up = lax.ppermute(got_up, "pair", swap)
        buf = store(buf, got_down, in_mine[0, t])
        buf = store(buf, got_up, in_mine[1, t])
        buf = store(buf, swap_down, in_sib[0, t])
        return store(buf, swap_up, in_sib[1, t])

    def step(t, carry):
        buf, send_down, send_up, got_down, got_up, out, done = carry
        next_down = lax.ppermute(send_down, "store", down)
        next_up = lax.ppermute(send_up, "store", up)
        buf = take_in(jnp.where(t > 0, t - 1, most - 1), buf, got_down, got_up)
        send_down = load(buf, out_mine[0, t + 1])
        send_up = load(buf, out_mine[1, t + 1])
        work = jnp.clip(ready_count[t] - done, 0, SLOTS_PER_STEP)
        span = jnp.stack([done, work, counts[0]])
        out = attend(SLOTS_PER_STEP, br, span, order, place, count_links, rows, q, buf, out)
        return buf, send_down, send_up, next_down, next_up, out, done + work

    send_down, send_up = load(buf, out_mine[0, 0]), load(buf, out_mine[1, 0])
    carry = (buf, send_down, send_up, send_down, send_up, out, jnp.int32(0))
    buf, _, _, got_down, got_up, out, done = lax.fori_loop(0, total, step, carry)
    buf = take_in(jnp.where(total > 0, total - 1, most - 1), buf, got_down, got_up)
    span = jnp.stack([done, slots - done, counts[0]])
    out = attend(slots, br, span, order, place, count_links, rows, q, buf, out)
    out = out[:slots].reshape(slots, kv_heads, br, group_size, depth)
    return jnp.transpose(out, (0, 2, 1, 3, 4)).reshape(queries.shape)


def solution(mesh):
    return jax.shard_map(
        local,
        mesh=mesh,
        in_specs=(
            P(("groups", "store", "pair"), "head", None, None, None),
            P(("groups", "store", "pair"), None, None, "head", None),
            P("groups"),
            P(("groups", "store", "pair"), None),
            P(("groups", "store", "pair")),
            P(("groups", "store", "pair"), None, None),
            P(("groups", "store", "pair"), None, None),
        ),
        out_specs=P(("groups", "store", "pair"), None, None, "head", None),
        check_vma=False,
    )
```

```python
import functools

import jax
import jax.numpy as jnp
from jax import lax
from jax.experimental import pallas as pl
from jax.experimental.pallas import tpu as pltpu
from jax.sharding import PartitionSpec as P

SLOTS_PER_STEP = 4
VMEM_BYTES = 48 * 1024 * 1024


def blank_kernel(out_ref):
    pass


def blank(shape, dtype):
    return pl.pallas_call(
        blank_kernel,
        out_shape=jax.ShapeDtypeStruct(shape, dtype),
        out_specs=pl.BlockSpec(memory_space=pl.ANY),
    )()


def attend_kernel(br, now, spans, order, place, extra, rows, q_ref, own_ref, one_ref, two_ref, prev_ref, out_ref):
    heads, total_rows, depth = q_ref.shape[1:]
    group = total_rows // br
    length = own_ref.shape[3]
    scale = depth ** (-0.5)
    step = pl.program_id(0)
    base = now[0] * 3
    index = spans[base] + step
    active = step < spans[base + 1]
    slot = order[jnp.minimum(index, order.shape[0] - 1)]
    live = jnp.logical_and(active, index < spans[base + 2])
    links = extra[slot]

    def run(kv_refs):
        position = lax.broadcasted_iota(jnp.int32, (group, length), 1)
        allowed = jnp.concatenate(
            [(position <= rows[slot * br + b]).astype(jnp.int32) for b in range(br)], axis=0
        ) > 0
        for h in range(heads):
            query = q_ref[0, h]
            scores = [
                lax.dot_general(
                    query, ref[0, h, 0], (((1,), (1,)), ((), ())), preferred_element_type=jnp.float32
                )
                for ref in kv_refs
            ]
            scores[0] = jnp.where(allowed, scores[0], -jnp.inf)
            peak = functools.reduce(jnp.maximum, scores)
            peak = jnp.max(peak, axis=1, keepdims=True)
            expon = [jnp.exp((s - peak) * scale) for s in scores]
            totals = jnp.sum(functools.reduce(jnp.add, expon), axis=1, keepdims=True)
            mixed = functools.reduce(
                jnp.add,
                [
                    jnp.dot(e.astype(jnp.bfloat16), ref[0, h, 1], preferred_element_type=jnp.float32)
                    for e, ref in zip(expon, kv_refs)
                ],
            )
            out_ref[0, h] = (mixed / totals).astype(out_ref.dtype)

    @pl.when(jnp.logical_and(live, links == 0))
    def _():
        run([own_ref])

    @pl.when(jnp.logical_and(live, links == 1))
    def _():
        run([own_ref, one_ref])

    @pl.when(jnp.logical_and(live, links == 2))
    def _():
        run([own_ref, one_ref, two_ref])

    @pl.when(jnp.logical_and(active, jnp.logical_not(live)))
    def _():
        out_ref[...] = jnp.zeros_like(out_ref)


def attend(steps, br, now, spans, order, place, extra, rows, q, buf, prev):
    slots, heads, total_rows, depth = q.shape
    kv_block = (1,) + buf.shape[1:]

    def pick(k, now, spans, order):
        base = now[0] * 3
        index = jnp.minimum(spans[base] + jnp.minimum(k, spans[base + 1] - 1), spans[base + 2] - 1)
        return order[jnp.clip(index, 0, slots - 1)]

    def q_map(k, now, spans, order, place, extra, rows):
        return (pick(k, now, spans, order), 0, 0, 0)

    def kv_map(which, k, now, spans, order, place, extra, rows):
        return (place[pick(k, now, spans, order) * 3 + which], 0, 0, 0, 0)

    def out_map(k, now, spans, order, place, extra, rows):
        base = now[0] * 3
        index = jnp.clip(spans[base] + k, 0, slots - 1)
        return (jnp.where(k < spans[base + 1], order[index], slots), 0, 0, 0)

    return pl.pallas_call(
        functools.partial(attend_kernel, br),
        out_shape=jax.ShapeDtypeStruct(prev.shape, prev.dtype),
        grid_spec=pltpu.PrefetchScalarGridSpec(
            num_scalar_prefetch=6,
            grid=(steps,),
            in_specs=[pl.BlockSpec((1, heads, total_rows, depth), q_map)]
            + [pl.BlockSpec(kv_block, functools.partial(kv_map, w)) for w in range(3)]
            + [pl.BlockSpec(memory_space=pl.ANY)],
            out_specs=pl.BlockSpec((1, heads, total_rows, depth), out_map),
        ),
        input_output_aliases={10: 0},
        compiler_params=pltpu.CompilerParams(
            dimension_semantics=("arbitrary",), vmem_limit_bytes=VMEM_BYTES
        ),
        cost_estimate=pl.CostEstimate(
            flops=4 * steps * heads * total_rows * 3 * buf.shape[3] * depth,
            bytes_accessed=steps * 4 * heads * buf.shape[3] * depth * 6,
            transcendentals=steps * heads * total_rows * 3 * buf.shape[3],
        ),
    )(now, spans, order, place, extra, rows, q, buf, buf, buf, prev)


def plan_links(need, held):
    chips = need.shape[2]
    dst = jnp.arange(chips)[:, None]
    src = jnp.arange(chips)[None, :]
    gap = jnp.where(src > dst, src - dst, 0)
    reach = jnp.max(jnp.where(need, gap[None, None, :, :, None, None], 0), axis=2)
    reach = jnp.swapaxes(reach, 2, 3)
    row = jnp.arange(held)
    ahead = (reach[..., None, :] > reach[..., :, None]) | (
        (reach[..., None, :] == reach[..., :, None]) & (row[None, :] < row[:, None])
    )
    rank = jnp.sum(ahead.astype(jnp.int32), axis=-1)
    start = jnp.zeros(reach.shape[:3] + (chips, chips), jnp.int32)
    last = None
    ends = []
    for d in range(1, chips):
        if last is None:
            now = jnp.zeros(reach.shape[:3] + (chips - 1,), jnp.int32)
        else:
            before = jnp.sum((reach >= d - 1).astype(jnp.int32), axis=-1)
            now = jnp.maximum(last[..., :-1] + before[..., d - 1 : chips - 1], last[..., 1:] + 1)
        sent = jnp.sum((reach >= d).astype(jnp.int32), axis=-1)[..., d:]
        ends.append(jnp.max(jnp.where(sent > 0, now + sent, 0)))
        wide = jnp.pad(now, [(0, 0)] * 3 + [(0, d)])
        start = jnp.where(src - dst == d, wide[..., :, None], start)
        last = now
    total = functools.reduce(jnp.maximum, ends, jnp.int32(0))
    time = start[..., None] + rank[:, :, :, None]
    used = (src > dst)[:, :, None] & (reach[:, :, :, None] >= (src - dst)[:, :, None])
    return jnp.where(used, time, -1), total


def local(passage_cache, queries, passage_home, retrieval, counts, boundary_rows, cross_blocks):
    groups = lax.axis_size("groups")
    chips = lax.axis_size("store")
    lanes = lax.axis_size("pair")
    my_group = lax.axis_index("groups")
    my_chip = lax.axis_index("store")
    my_lane = lax.axis_index("pair")
    held = passage_cache.shape[0]
    passages = passage_home.shape[0]
    slots = retrieval.shape[1]
    br = queries.shape[2]
    kv_heads = passage_cache.shape[1]
    group_size = queries.shape[3] // kv_heads
    depth = queries.shape[4]
    swap = [(i, (i + 1) % lanes) for i in range(lanes)]
    down = [(i + 1, i) for i in range(chips - 1)]
    up = [(i, i + 1) for i in range(chips - 1)]

    sibling = lax.ppermute(passage_cache, "pair", swap)
    my_shard = my_chip * lanes + my_lane
    sib_shard = my_chip * lanes + (my_lane + 1) % lanes
    buf = blank((passages + 1,) + passage_cache.shape[1:], passage_cache.dtype)
    buf = lax.dynamic_update_slice_in_dim(buf, passage_cache, my_shard * held, 0)
    buf = lax.dynamic_update_slice_in_dim(buf, sibling, sib_shard * held, 0)

    slot_ids = jnp.arange(slots, dtype=jnp.int32)
    live = slot_ids < counts[0]
    places = passage_home[retrieval[0]]
    hit = live[:, None] & (places[:, None] == jnp.arange(passages, dtype=jnp.int32)[None, :])
    needed = jnp.any(hit, axis=0).astype(jnp.int32)
    every = lax.all_gather(needed[None], ("groups", "store", "pair"), axis=0, tiled=True)
    need = jnp.max(every.reshape(groups, chips, lanes, passages), axis=2) > 0
    need = need.reshape(groups, chips, chips, lanes, held)
    time, total = plan_links(jnp.stack([need, need[:, ::-1, ::-1]]), held)

    my_time = lax.dynamic_index_in_dim(time, my_group, 1, keepdims=False)
    line = jnp.stack([my_chip, chips - 1 - my_chip])
    padded = jnp.pad(my_time, [(0, 0), (0, 0), (1, 0), (0, 0), (0, 0)], constant_values=-1)
    at_link = jnp.arange(chips + 1, dtype=jnp.int32)[None, :]
    select_in = (at_link == line[:, None] + 1)[:, None, :, None, None]
    select_out = (at_link == line[:, None])[:, None, :, None, None]
    time_in = jnp.max(jnp.where(select_in, padded, -1), axis=2)
    time_out = jnp.max(jnp.where(select_out, padded, -1), axis=2)
    home = jnp.arange(chips, dtype=jnp.int32)
    home = jnp.stack([home, chips - 1 - home])
    row_id = (
        (home[:, None, :, None] * lanes + jnp.arange(lanes, dtype=jnp.int32)[None, :, None, None]) * held
        + jnp.arange(held, dtype=jnp.int32)
    )
    most = (chips - 1) * held + 2
    steps = jnp.arange(most, dtype=jnp.int32)

    def table(when, empty):
        found = when[..., None] == steps
        value = jnp.sum(jnp.where(found, row_id[..., None] + 1, 0), axis=(2, 3)) - 1
        return jnp.where(value >= 0, value, empty)

    row_in = table(time_in, passages)
    row_out = table(time_out, my_shard * held)
    in_mine = lax.dynamic_index_in_dim(row_in, my_lane, 1, keepdims=False)
    in_sib = lax.dynamic_index_in_dim(row_in, (my_lane + 1) % lanes, 1, keepdims=False)
    out_mine = lax.dynamic_index_in_dim(row_out, my_lane, 1, keepdims=False)

    links = cross_blocks[0]
    valid = links != slot_ids[:, None]
    first = jnp.where(valid[:, 0], links[:, 0], links[:, 1])
    second = links[:, 1]
    count_links = jnp.sum(valid.astype(jnp.int32), axis=1)
    first = jnp.where(count_links >= 1, first, slot_ids)
    second = jnp.where(count_links >= 2, second, first)
    members = jnp.stack([slot_ids, first, second], axis=1)
    member_hit = (members[:, :, None] == slot_ids[None, None, :]) & live[None, None, :]
    member_place = jnp.sum(jnp.where(member_hit, places[None, None, :], 0), axis=2)
    arrival = jnp.max(
        jnp.where(
            (row_id[..., None] == jnp.arange(passages, dtype=jnp.int32)), time_in[..., None] + 1, 0
        ),
        axis=(0, 1, 2, 3),
    )
    slot_arrival = jnp.sum(jnp.where(hit, arrival[None, :], 0), axis=1)
    ready = jnp.max(jnp.where(member_hit, slot_arrival[None, None, :], 0), axis=(1, 2))
    ready = jnp.where(live, ready, most + 2)
    sooner = (ready[None, :] < ready[:, None]) | (
        (ready[None, :] == ready[:, None]) & (slot_ids[None, :] < slot_ids[:, None])
    )
    rank = jnp.sum(sooner.astype(jnp.int32), axis=1)
    order = jnp.sum(jnp.where(rank[None, :] == slot_ids[:, None], slot_ids[None, :], 0), axis=1)
    ready_count = jnp.sum((ready[None, :] <= steps[:, None]).astype(jnp.int32), axis=1)

    q = queries[0].reshape(slots, br, kv_heads, group_size, depth)
    q = jnp.transpose(q, (0, 2, 1, 3, 4)).reshape(slots, kv_heads, br * group_size, depth)
    rows = boundary_rows[0].reshape(-1)
    place = member_place.reshape(-1)
    out = blank((slots + 1,) + q.shape[1:], q.dtype)

    lag = steps[:, None] - steps[None, :]
    done = jnp.where(lag > 0, ready_count[None, :] + SLOTS_PER_STEP * (lag - 1), slots)
    done = jnp.minimum(jnp.min(done, axis=1), SLOTS_PER_STEP * steps)
    work = jnp.clip(ready_count - done, 0, SLOTS_PER_STEP)
    work = jnp.where(steps == total, slots - done, work)
    spans = jnp.stack([done, work, jnp.broadcast_to(counts[0], done.shape)], axis=1).reshape(-1)

    def late(rows):
        return jnp.concatenate([jnp.full_like(rows[:, :1], passages), rows[:, :-1]], axis=1)

    moves = jnp.concatenate([out_mine, in_mine, late(in_mine), late(in_sib)], axis=0).astype(jnp.uint32)
    zero = jnp.uint32(0)
    tail = (zero,) * (passage_cache.ndim - 1)
    block = (1,) + passage_cache.shape[1:]

    def store(buf, value, row):
        return lax.dynamic_update_slice(buf, value, (row,) + tail)

    def load(buf, row):
        return lax.dynamic_slice(buf, (row,) + tail, block)

    def share(buf, row):
        down_block, up_block, buf = lax.optimization_barrier((load(buf, row[4]), load(buf, row[5]), buf))
        down_block = lax.ppermute(down_block, "pair", swap)
        up_block = lax.ppermute(up_block, "pair", swap)
        return store(store(buf, down_block, row[6]), up_block, row[7])

    def step(t, carry):
        buf, out = carry
        row = lax.dynamic_slice(moves, (zero, t), (8, 1))[:, 0]
        got_down, got_up, buf = lax.optimization_barrier((load(buf, row[0]), load(buf, row[1]), buf))
        got_down = lax.ppermute(got_down, "store", down)
        got_up = lax.ppermute(got_up, "store", up)
        buf = share(buf, row)
        now = t.astype(jnp.int32).reshape(1)
        out = attend(SLOTS_PER_STEP, br, now, spans, order, place, count_links, rows, q, buf, out)
        buf, out, got_down, got_up = lax.optimization_barrier((buf, out, got_down, got_up))
        buf = store(store(buf, got_down, row[2]), got_up, row[3])
        return buf, out

    buf, out = lax.fori_loop(zero, total.astype(jnp.uint32), step, (buf, out))
    row = lax.dynamic_slice(moves, (zero, total.astype(jnp.uint32)), (8, 1))[:, 0]
    buf = share(buf, row)
    out = attend(slots, br, total.reshape(1), spans, order, place, count_links, rows, q, buf, out)
    out = out[:slots].reshape(slots, kv_heads, br, group_size, depth)
    return jnp.transpose(out, (0, 2, 1, 3, 4)).reshape(queries.shape)


def solution(mesh):
    return jax.shard_map(
        local,
        mesh=mesh,
        in_specs=(
            P(("groups", "store", "pair"), "head", None, None, None),
            P(("groups", "store", "pair"), None, None, "head", None),
            P("groups"),
            P(("groups", "store", "pair"), None),
            P(("groups", "store", "pair")),
            P(("groups", "store", "pair"), None, None),
            P(("groups", "store", "pair"), None, None),
        ),
        out_specs=P(("groups", "store", "pair"), None, None, "head", None),
        check_vma=False,
    )
```

```python
import functools

import jax
import jax.numpy as jnp
from jax import lax
from jax.experimental import pallas as pl
from jax.experimental.pallas import tpu as pltpu
from jax.sharding import PartitionSpec as P

VMEM_BYTES = 48 * 1024 * 1024


def blank_kernel(out_ref):
    pass


def blank(shape, dtype):
    return pl.pallas_call(
        blank_kernel,
        out_shape=jax.ShapeDtypeStruct(shape, dtype),
        out_specs=pl.BlockSpec(memory_space=pl.ANY),
    )()


def attend_kernel(br, now, spans, order, place, extra, rows, q_ref, own_ref, one_ref, two_ref, prev_ref, out_ref):
    heads, total_rows, depth = q_ref.shape[1:]
    group = total_rows // br
    length = own_ref.shape[3]
    scale = depth ** (-0.5)
    step = pl.program_id(0)
    base = now[0] * 3
    index = spans[base] + step
    active = step < spans[base + 1]
    slot = order[jnp.minimum(index, order.shape[0] - 1)]
    live = jnp.logical_and(active, index < spans[base + 2])
    links = extra[slot]

    def run(kv_refs):
        position = lax.broadcasted_iota(jnp.int32, (group, length), 1)
        allowed = jnp.concatenate(
            [(position <= rows[slot * br + b]).astype(jnp.int32) for b in range(br)], axis=0
        ) > 0
        for h in range(heads):
            query = q_ref[0, h]
            scores = [
                lax.dot_general(
                    query, ref[0, h, 0], (((1,), (1,)), ((), ())), preferred_element_type=jnp.float32
                )
                for ref in kv_refs
            ]
            scores[0] = jnp.where(allowed, scores[0], -jnp.inf)
            peak = functools.reduce(jnp.maximum, scores)
            peak = jnp.max(peak, axis=1, keepdims=True)
            expon = [jnp.exp((s - peak) * scale) for s in scores]
            totals = jnp.sum(functools.reduce(jnp.add, expon), axis=1, keepdims=True)
            mixed = functools.reduce(
                jnp.add,
                [
                    jnp.dot(e.astype(jnp.bfloat16), ref[0, h, 1], preferred_element_type=jnp.float32)
                    for e, ref in zip(expon, kv_refs)
                ],
            )
            out_ref[0, h] = (mixed / totals).astype(out_ref.dtype)

    @pl.when(jnp.logical_and(live, links == 0))
    def _():
        run([own_ref])

    @pl.when(jnp.logical_and(live, links == 1))
    def _():
        run([own_ref, one_ref])

    @pl.when(jnp.logical_and(live, links == 2))
    def _():
        run([own_ref, one_ref, two_ref])

    @pl.when(jnp.logical_and(active, jnp.logical_not(live)))
    def _():
        out_ref[...] = jnp.zeros_like(out_ref)


def attend(steps, br, now, spans, order, place, extra, rows, q, buf, prev):
    slots, heads, total_rows, depth = q.shape
    kv_block = (1,) + buf.shape[1:]

    def pick(k, now, spans, order):
        base = now[0] * 3
        index = jnp.minimum(spans[base] + jnp.minimum(k, spans[base + 1] - 1), spans[base + 2] - 1)
        return order[jnp.clip(index, 0, slots - 1)]

    def q_map(k, now, spans, order, place, extra, rows):
        return (pick(k, now, spans, order), 0, 0, 0)

    def kv_map(which, k, now, spans, order, place, extra, rows):
        return (place[pick(k, now, spans, order) * 3 + which], 0, 0, 0, 0)

    def out_map(k, now, spans, order, place, extra, rows):
        base = now[0] * 3
        index = jnp.clip(spans[base] + k, 0, slots - 1)
        return (jnp.where(k < spans[base + 1], order[index], slots), 0, 0, 0)

    return pl.pallas_call(
        functools.partial(attend_kernel, br),
        out_shape=jax.ShapeDtypeStruct(prev.shape, prev.dtype),
        grid_spec=pltpu.PrefetchScalarGridSpec(
            num_scalar_prefetch=6,
            grid=(steps,),
            in_specs=[pl.BlockSpec((1, heads, total_rows, depth), q_map)]
            + [pl.BlockSpec(kv_block, functools.partial(kv_map, w)) for w in range(3)]
            + [pl.BlockSpec(memory_space=pl.ANY)],
            out_specs=pl.BlockSpec((1, heads, total_rows, depth), out_map),
        ),
        input_output_aliases={10: 0},
        compiler_params=pltpu.CompilerParams(
            dimension_semantics=("arbitrary",), vmem_limit_bytes=VMEM_BYTES
        ),
        cost_estimate=pl.CostEstimate(
            flops=4 * steps * heads * total_rows * 3 * buf.shape[3] * depth,
            bytes_accessed=steps * 4 * heads * buf.shape[3] * depth * 6,
            transcendentals=steps * heads * total_rows * 3 * buf.shape[3],
        ),
    )(now, spans, order, place, extra, rows, q, buf, buf, buf, prev)


def local(passage_cache, queries, passage_home, retrieval, counts, boundary_rows, cross_blocks):
    slots = retrieval.shape[1]
    br = queries.shape[2]
    kv_heads = passage_cache.shape[1]
    group_size = queries.shape[3] // kv_heads
    depth = queries.shape[4]
    slot_ids = jnp.arange(slots, dtype=jnp.int32)
    live = slot_ids < counts[0]
    places = passage_home[retrieval[0]]

    links = cross_blocks[0]
    valid = links != slot_ids[:, None]
    count_links = jnp.sum(valid.astype(jnp.int32), axis=1)
    first = jnp.where(valid[:, 0], links[:, 0], links[:, 1])
    first = jnp.where(count_links >= 1, first, slot_ids)
    second = jnp.where(count_links >= 2, links[:, 1], first)
    members = jnp.stack([slot_ids, first, second], axis=1)
    member_hit = (members[:, :, None] == slot_ids[None, None, :]) & live[None, None, :]
    place = jnp.sum(jnp.where(member_hit, places[None, None, :], 0), axis=2).reshape(-1)
    rows = boundary_rows[0].reshape(-1)
    now = jnp.zeros((1,), jnp.int32)
    spans = jnp.stack([jnp.int32(0), jnp.int32(slots), counts[0]])

    cuts = [(0, kv_heads - 1), (kv_heads - 1, kv_heads)] if kv_heads > 1 else [(0, kv_heads)]
    q = queries[0].reshape(slots, br, kv_heads, group_size, depth)
    parts = []
    gathered = None
    for low, high in cuts:
        piece = passage_cache[:, low:high]
        if gathered is not None:
            piece, gathered = lax.optimization_barrier((piece, gathered))
            parts.append((gathered,) + parts.pop()[1:])
        gathered = lax.all_gather(piece, ("store", "pair"), axis=0, tiled=True)
        q_part = jnp.transpose(q[:, :, low:high], (0, 2, 1, 3, 4))
        parts.append((gathered, q_part.reshape(slots, high - low, br * group_size, depth)))
    outs = []
    for kv, q_part in parts:
        out = blank((slots + 1,) + q_part.shape[1:], q.dtype)
        out = attend(slots, br, now, spans, slot_ids, place, count_links, rows, q_part, kv, out)
        out = out[:slots].reshape(slots, q_part.shape[1], br, group_size, depth)
        outs.append(jnp.transpose(out, (0, 2, 1, 3, 4)))
    return jnp.concatenate(outs, axis=2).reshape(queries.shape)


def solution(mesh):
    return jax.shard_map(
        local,
        mesh=mesh,
        in_specs=(
            P(("groups", "store", "pair"), "head", None, None, None),
            P(("groups", "store", "pair"), None, None, "head", None),
            P("groups"),
            P(("groups", "store", "pair"), None),
            P(("groups", "store", "pair")),
            P(("groups", "store", "pair"), None, None),
            P(("groups", "store", "pair"), None, None),
        ),
        out_specs=P(("groups", "store", "pair"), None, None, "head", None),
        check_vma=False,
    )
```

```python
import functools

import jax
import jax.numpy as jnp
from jax import lax
from jax.experimental import pallas as pl
from jax.experimental.pallas import tpu as pltpu
from jax.sharding import PartitionSpec as P

VMEM_BYTES = 48 * 1024 * 1024


def blank_kernel(out_ref):
    pass


def blank(shape, dtype):
    return pl.pallas_call(
        blank_kernel,
        out_shape=jax.ShapeDtypeStruct(shape, dtype),
        out_specs=pl.BlockSpec(memory_space=pl.ANY),
    )()


def attend_kernel(br, now, spans, order, place, extra, rows, q_ref, own_ref, one_ref, two_ref, prev_ref, out_ref):
    heads, total_rows, depth = q_ref.shape[1:]
    group = total_rows // br
    length = own_ref.shape[3]
    scale = depth ** (-0.5)
    step = pl.program_id(0)
    base = now[0] * 3
    index = spans[base] + step
    active = step < spans[base + 1]
    slot = order[jnp.minimum(index, order.shape[0] - 1)]
    live = jnp.logical_and(active, index < spans[base + 2])
    links = extra[slot]

    def run(kv_refs):
        position = lax.broadcasted_iota(jnp.int32, (group, length), 1)
        allowed = jnp.concatenate(
            [(position <= rows[slot * br + b]).astype(jnp.int32) for b in range(br)], axis=0
        ) > 0
        cuts = 2 if heads == 1 and total_rows % 32 == 0 else 1
        part = total_rows // cuts
        for h, c in [(h, c) for h in range(heads) for c in range(cuts)]:
            span_rows = slice(c * part, (c + 1) * part)
            query = q_ref[0, h, span_rows]
            scores = [
                lax.dot_general(
                    query, ref[0, h, 0], (((1,), (1,)), ((), ())), preferred_element_type=jnp.float32
                )
                for ref in kv_refs
            ]
            scores[0] = jnp.where(allowed[span_rows], scores[0], -jnp.inf)
            peak = functools.reduce(jnp.maximum, scores)
            peak = jnp.max(peak, axis=1, keepdims=True)
            expon = [jnp.exp((s - peak) * scale) for s in scores]
            totals = jnp.sum(functools.reduce(jnp.add, expon), axis=1, keepdims=True)
            mixed = functools.reduce(
                jnp.add,
                [
                    jnp.dot(e.astype(jnp.bfloat16), ref[0, h, 1], preferred_element_type=jnp.float32)
                    for e, ref in zip(expon, kv_refs)
                ],
            )
            out_ref[0, h, span_rows] = (mixed / totals).astype(out_ref.dtype)

    @pl.when(jnp.logical_and(live, links == 0))
    def _():
        run([own_ref])

    @pl.when(jnp.logical_and(live, links == 1))
    def _():
        run([own_ref, one_ref])

    @pl.when(jnp.logical_and(live, links == 2))
    def _():
        run([own_ref, one_ref, two_ref])

    @pl.when(jnp.logical_and(active, jnp.logical_not(live)))
    def _():
        out_ref[...] = jnp.zeros_like(out_ref)


def attend(steps, br, now, spans, order, place, extra, rows, q, buf, prev):
    slots, heads, total_rows, depth = q.shape
    kv_block = (1,) + buf.shape[1:]

    def pick(k, now, spans, order):
        base = now[0] * 3
        index = jnp.minimum(spans[base] + jnp.minimum(k, spans[base + 1] - 1), spans[base + 2] - 1)
        return order[jnp.clip(index, 0, slots - 1)]

    def q_map(k, now, spans, order, place, extra, rows):
        return (pick(k, now, spans, order), 0, 0, 0)

    def kv_map(which, k, now, spans, order, place, extra, rows):
        return (place[pick(k, now, spans, order) * 3 + which], 0, 0, 0, 0)

    def out_map(k, now, spans, order, place, extra, rows):
        base = now[0] * 3
        index = jnp.clip(spans[base] + k, 0, slots - 1)
        return (jnp.where(k < spans[base + 1], order[index], slots), 0, 0, 0)

    return pl.pallas_call(
        functools.partial(attend_kernel, br),
        out_shape=jax.ShapeDtypeStruct(prev.shape, prev.dtype),
        grid_spec=pltpu.PrefetchScalarGridSpec(
            num_scalar_prefetch=6,
            grid=(steps,),
            in_specs=[pl.BlockSpec((1, heads, total_rows, depth), q_map)]
            + [pl.BlockSpec(kv_block, functools.partial(kv_map, w)) for w in range(3)]
            + [pl.BlockSpec(memory_space=pl.ANY)],
            out_specs=pl.BlockSpec((1, heads, total_rows, depth), out_map),
        ),
        input_output_aliases={10: 0},
        compiler_params=pltpu.CompilerParams(
            dimension_semantics=("arbitrary",), vmem_limit_bytes=VMEM_BYTES
        ),
        cost_estimate=pl.CostEstimate(
            flops=4 * steps * heads * total_rows * 3 * buf.shape[3] * depth,
            bytes_accessed=steps * 4 * heads * buf.shape[3] * depth * 6,
            transcendentals=steps * heads * total_rows * 3 * buf.shape[3],
        ),
    )(now, spans, order, place, extra, rows, q, buf, buf, buf, prev)


def local(passage_cache, queries, passage_home, retrieval, counts, boundary_rows, cross_blocks):
    slots = retrieval.shape[1]
    br = queries.shape[2]
    kv_heads = passage_cache.shape[1]
    group_size = queries.shape[3] // kv_heads
    depth = queries.shape[4]
    slot_ids = jnp.arange(slots, dtype=jnp.int32)
    live = slot_ids < counts[0]
    places = passage_home[retrieval[0]]

    links = cross_blocks[0]
    valid = links != slot_ids[:, None]
    count_links = jnp.sum(valid.astype(jnp.int32), axis=1)
    first = jnp.where(valid[:, 0], links[:, 0], links[:, 1])
    first = jnp.where(count_links >= 1, first, slot_ids)
    second = jnp.where(count_links >= 2, links[:, 1], first)
    members = jnp.stack([slot_ids, first, second], axis=1)
    member_hit = (members[:, :, None] == slot_ids[None, None, :]) & live[None, None, :]
    place = jnp.sum(jnp.where(member_hit, places[None, None, :], 0), axis=2).reshape(-1)
    rows = boundary_rows[0].reshape(-1)
    now = jnp.zeros((1,), jnp.int32)
    spans = jnp.stack([jnp.int32(0), jnp.int32(slots), counts[0]])

    cuts = [(0, kv_heads - 1), (kv_heads - 1, kv_heads)] if kv_heads > 1 else [(0, kv_heads)]
    q = queries[0].reshape(slots, br, kv_heads, group_size, depth)
    parts = []
    gathered = None
    for low, high in cuts:
        piece = passage_cache[:, low:high]
        if gathered is not None:
            piece, gathered = lax.optimization_barrier((piece, gathered))
            parts.append((gathered,) + parts.pop()[1:])
        gathered = lax.all_gather(piece, ("store", "pair"), axis=0, tiled=True)
        q_part = jnp.transpose(q[:, :, low:high], (0, 2, 1, 3, 4))
        parts.append((gathered, q_part.reshape(slots, high - low, br * group_size, depth)))
    outs = []
    for kv, q_part in parts:
        out = blank((slots + 1,) + q_part.shape[1:], q.dtype)
        out = attend(slots, br, now, spans, slot_ids, place, count_links, rows, q_part, kv, out)
        out = out[:slots].reshape(slots, q_part.shape[1], br, group_size, depth)
        outs.append(jnp.transpose(out, (0, 2, 1, 3, 4)))
    return jnp.concatenate(outs, axis=2).reshape(queries.shape)


def solution(mesh):
    return jax.shard_map(
        local,
        mesh=mesh,
        in_specs=(
            P(("groups", "store", "pair"), "head", None, None, None),
            P(("groups", "store", "pair"), None, None, "head", None),
            P("groups"),
            P(("groups", "store", "pair"), None),
            P(("groups", "store", "pair")),
            P(("groups", "store", "pair"), None, None),
            P(("groups", "store", "pair"), None, None),
        ),
        out_specs=P(("groups", "store", "pair"), None, None, "head", None),
        check_vma=False,
    )
```
